128 devices in a mesh: gx: 4 (over y), gy: 4 (over x_hi, core), gz: 8 (over x_lo, z).
Axes of the slice: x: 4 (x_hi: 2, x_lo: 2; x = x_hi * 2 + x_lo), y: 4, z: 4, core: 2. Of those that a mesh axis runs over, the one named last changes fastest.
Arguments:
- tokens: bfloat16 [64, 64, 128, 256], P('gx', 'gy', 'gz'), may hold values from -17 to 17, as said below
- grad_out: bfloat16 [64, 64, 128, 256], P('gx', 'gy', 'gz'), may hold values from -6 to 6
- w_qkv: bfloat16 [256, 768], replicated, may hold values from -0.375 to 0.375
- w_out: bfloat16 [256, 256], replicated, may hold values from -0.375 to 0.375
Outputs:
- grad_tokens: bfloat16 [64, 64, 128, 256], P('gx', 'gy', 'gz')
- grad_qkv_weight: float32 [256, 768], replicated
- grad_out_weight: float32 [256, 256], replicated
The draws below stay inside these ranges and needn't reach their ends.
Inputs may be any that keep to these rules, and one draw needn't show every extreme that they name: `tokens`: entries of order one, each token row multiplied by its own positive scale.
All inputs are finite; a program needn't handle non-finite values.
Results may differ from the reference program's by a relative error of at most 0.015.
Values may be sent and summed in bfloat16 or wider, within the bound.
A program may use at most 128 MiB of HBM per device.

```python
import math
import jax
import jax.numpy as jnp
from jax import lax

HEADS = 8
HEAD_DIM = 32
D = 256
GRID = 4
NX = 64
NY = 64
NZ = 128


def draw_tokens(key, part):
    key = jax.random.fold_in(key, 11)
    first, second = jax.random.split(key)
    entries = jnp.clip(jax.random.normal(first, (NX, NY, NZ, D), jnp.float32), -6.0, 6.0)
    spread = jax.random.uniform(second, (NX, NY, NZ, 1), jnp.float32, math.log(0.5), math.log(2.0))
    return (entries * jnp.exp(spread)).astype(jnp.bfloat16)


def block_levels(key, extent, cuts, least, high):
    def one(position, shards_of):
        draws = jax.random.uniform(jax.random.fold_in(jax.random.fold_in(key, 6), position), (shards_of,), jnp.float32, least / len(cuts), high / len(cuts))
        return jnp.repeat(jnp.exp(draws), extent[position] // shards_of).reshape((-1,) + (1,) * (len(extent) - position - 1))

    factor_of = one(*cuts[0])
    for cut in cuts[1:]:
        factor_of = factor_of * one(*cut)
    return factor_of


def centred(key, dims, scale, reach, cuts=(), dtype=jnp.bfloat16):
    factor_of = block_levels(key, dims, cuts, -0.22, 0.18) if cuts else 1.0
    result = jax.random.normal(key, dims, jnp.float32) * scale * factor_of
    return jnp.minimum(jnp.maximum(result, -reach), reach).astype(dtype)


def setup_inputs(seed: int = 0) -> dict:
    key_list = jax.random.split(jax.random.key(seed), 5)
    return {
        "tokens": draw_tokens(jax.random.fold_in(key_list[4], 71), 0),
        "grad_out": centred(key_list[1], (NX, NY, NZ, D), 1.0, 6.0, ((0, 4), (1, 4), (2, 8))),
        "w_qkv": centred(key_list[2], (D, 3 * D), D ** -0.5, 0.375),
        "w_out": centred(key_list[3], (D, D), D ** -0.5, 0.375),
    }


def to_windows(arranged):
    size_x, size_y, size_z, width = arranged.shape
    arranged = arranged.reshape(GRID, size_x // GRID, GRID, size_y // GRID, GRID, size_z // GRID, width)
    arranged = arranged.transpose(1, 3, 5, 0, 2, 4, 6)
    return arranged.reshape(-1, GRID ** 3, width)


def from_windows(arranged, size_x, size_y, size_z):
    width = arranged.shape[-1]
    arranged = arranged.reshape(size_x // GRID, size_y // GRID, size_z // GRID, GRID, GRID, GRID, width)
    arranged = arranged.transpose(3, 0, 4, 1, 5, 2, 6)
    return arranged.reshape(size_x, size_y, size_z, width)


def window_backward(token_rows, grad_rows, w_qkv, w_out):
    count, members, width = token_rows.shape
    scaling = HEAD_DIM ** -0.5
    qkv = jnp.einsum("wmd,de->wme", token_rows.astype(jnp.float32), w_qkv.astype(jnp.float32)).astype(jnp.bfloat16)
    per_head = qkv.reshape(count, members, 3, HEADS, HEAD_DIM).astype(jnp.float32)
    queries, key_rows, values = per_head[:, :, 0], per_head[:, :, 1], per_head[:, :, 2]
    scores = jnp.einsum("wqhc,wkhc->whqk", queries, key_rows) * scaling
    attention = jax.nn.softmax(scores, axis=-1)
    attention_b = attention.astype(jnp.bfloat16).astype(jnp.float32)
    mixed = jnp.einsum("whqk,wkhc->wqhc", attention_b, values).astype(jnp.bfloat16)
    grad_mixed = jnp.einsum("wme,de->wmd", grad_rows.astype(jnp.float32), w_out.astype(jnp.float32)).astype(jnp.bfloat16)
    grad_heads = grad_mixed.reshape(count, members, HEADS, HEAD_DIM).astype(jnp.float32)
    weight_grad = jnp.einsum("wqhc,wkhc->whqk", grad_heads, values)
    inner = jnp.sum(attention * weight_grad, axis=-1, keepdims=True)
    score_grad = (attention * (weight_grad - inner) * scaling).astype(jnp.bfloat16).astype(jnp.float32)
    query_grad = jnp.einsum("whqk,wkhc->wqhc", score_grad, key_rows).astype(jnp.bfloat16)
    key_grad = jnp.einsum("whqk,wqhc->wkhc", score_grad, queries).astype(jnp.bfloat16)
    value_grad = jnp.einsum("whqk,wqhc->wkhc", attention_b, grad_heads).astype(jnp.bfloat16)
    qkv_grad = jnp.stack([query_grad, key_grad, value_grad], axis=2).reshape(count, members, 3 * width)
    qkv_grad_f = qkv_grad.astype(jnp.float32)
    token_grad = jnp.einsum("wme,de->wmd", qkv_grad_f, w_qkv.astype(jnp.float32)).astype(jnp.bfloat16)
    part_qkv = jnp.einsum("wmd,wme->de", token_rows.astype(jnp.float32), qkv_grad_f)
    mixed_rows = mixed.reshape(count, members, width).astype(jnp.float32)
    part_out = jnp.einsum("wmd,wme->de", mixed_rows, grad_rows.astype(jnp.float32))
    return token_grad, part_qkv, part_out


def reference(tokens, grad_out, w_qkv, w_out):
    size_x, size_y, size_z, width = tokens.shape
    token_win = to_windows(tokens)
    grad_win = to_windows(grad_out)
    total = token_win.shape[0]
    block = math.gcd(total, 64)
    rounds = total // block
    token_blocks = token_win.reshape(rounds, block, GRID ** 3, width)
    grad_blocks = grad_win.reshape(rounds, block, GRID ** 3, width)

    def one_block(carry, pieces):
        token_grad, part_qkv, part_out = window_backward(pieces[0], pieces[1], w_qkv, w_out)
        return (carry[0] + part_qkv, carry[1] + part_out), token_grad

    start = (jnp.zeros((width, 3 * width), jnp.float32), jnp.zeros((width, width), jnp.float32))
    (grad_qkv_weight, grad_out_weight), token_grads = lax.scan(one_block, start, (token_blocks, grad_blocks))
    grad_tokens = from_windows(token_grads.reshape(total, GRID ** 3, width), size_x, size_y, size_z)
    return grad_tokens, grad_qkv_weight, grad_out_weight
```

```python
import functools
import math

import jax
import jax.numpy as jnp
from jax import lax
from jax.experimental import pallas as pl
from jax.experimental.pallas import tpu as pltpu
from jax.sharding import PartitionSpec as P

BF = jnp.bfloat16
F32 = jnp.float32
MESH = pl.DeviceIdType.MESH
HD = 32
MEM = 64
WIN = 16
PARTS = 4
D = 256
NN = (((1,), (0,)), ((), ()))
NT = (((1,), (1,)), ((), ()))
TN = (((0,), (0,)), ((), ()))
SCALE = HD ** -0.5


def dot(a, b, dims=NN):
    return lax.dot_general(a, b, dims, preferred_element_type=F32)


def swap_matrix():
    row = lax.broadcasted_iota(jnp.int32, (256, 256), 0)
    col = lax.broadcasted_iota(jnp.int32, (256, 256), 1)
    return jnp.where((row % 16) * 16 + row // 16 == col, 1.0, 0.0).astype(BF)


def spread(rows):
    lane = lax.broadcasted_iota(jnp.int32, (MEM, 128), 1) // HD
    return jnp.concatenate([jnp.where(lane == h, rows, jnp.zeros_like(rows)) for h in range(4)], axis=0)


def gather_heads(wide):
    lane = lax.broadcasted_iota(jnp.int32, (MEM, 128), 1) // HD
    out = wide[3 * MEM:]
    for h in (2, 1, 0):
        out = jnp.where(lane == h, wide[h * MEM:(h + 1) * MEM], out)
    return out


def columns(hg):
    return [slice(b * D + hg * 128, b * D + hg * 128 + 128) for b in range(4)]


def stage1(w, qkvg, sbuf):
    for hg in range(2):
        q, k, v, g = (qkvg[w, :, s] for s in columns(hg))
        sbuf[0, hg] = dot(k, spread(q), NT)
        sbuf[1, hg] = dot(v, spread(g), NT)


def stage2(sbuf, pbuf):
    for hg in range(2):
        scores = sbuf[0, hg]
        top = jnp.max(scores, axis=0, keepdims=True)
        e = jnp.exp2((scores - top) * (SCALE * math.log2(math.e)))
        total = jnp.sum(e, axis=0, keepdims=True)
        att = e * (1.0 / total)
        wg = sbuf[1, hg]
        inner = jnp.sum(att * wg, axis=0, keepdims=True)
        pbuf[0, hg] = att.astype(BF)
        pbuf[1, hg] = (att * ((wg - inner) * SCALE)).astype(BF)


def stage3(w, qkvg, pbuf, mix, grads):
    for hg in range(2):
        s = columns(hg)
        q, k, v, g = (qkvg[w, :, part] for part in s)
        ab, sg = pbuf[0, hg], pbuf[1, hg]
        grads[w, :, s[2]] = dot(ab, spread(g)).astype(BF)
        grads[w, :, s[1]] = dot(sg, spread(q)).astype(BF)
        mix[w, :, s[0]] = gather_heads(dot(ab, v, TN)).astype(BF)
        grads[w, :, s[0]] = gather_heads(dot(sg, k, TN)).astype(BF)


def compute_part(arrived, leaving, swap, wqkv, wout, xw, gw, qkvg, grads, mix, dx, sbuf, pbuf, acc):
    for m in range(0, MEM, 16):
        rows = dot(swap, arrived[m:m + 16].reshape(256, 512)).astype(BF).reshape(WIN, 16, 512)
        xw[:, m:m + 16, :] = rows[:, :, :D]
        gw[:, m:m + 16, :] = rows[:, :, D:]

    x = xw[...].reshape(-1, D)
    g = gw[...].reshape(-1, D)
    qkvg[:, :, 0:3 * D] = dot(x, wqkv[...]).astype(BF).reshape(WIN, MEM, 3 * D)
    qkvg[:, :, 3 * D:] = dot(g, wout[...], NT).astype(BF).reshape(WIN, MEM, D)

    def step(i, carry):
        stage3(jnp.maximum(i - 2, 0), qkvg, pbuf, mix, grads)
        stage2(sbuf, pbuf)
        stage1(jnp.minimum(i, WIN - 1), qkvg, sbuf)
        return carry

    lax.fori_loop(0, WIN + 2, step, 0)

    gr = grads[...].reshape(-1, 3 * D)
    dx[...] = dot(gr, wqkv[...], NT).astype(BF).reshape(WIN, MEM, D)
    acc[:, 0:3 * D] += dot(xw[...].reshape(-1, D), gr, TN)
    acc[:, 3 * D:] += dot(mix[...].reshape(-1, D), gw[...].reshape(-1, D), TN)

    for m in range(0, MEM, 16):
        rows = dx[:, m:m + 16, :].reshape(256, D)
        leaving[m:m + 16] = dot(swap, rows).astype(BF).reshape(16, WIN, D)


def kernel(tok, grd, wqkv, wout, out, dwqkv, dwout, staged, arrived, leaving, swap, xw, gw, qkvg, grads, mix, dx, sbuf, pbuf,
           acc, accb, terms, half, pair, sums, gathered, stage_sem, go_sem, come_sem, back_sem, land_sem, dw_sem):
    y, gy, gz = lax.axis_index("gx"), lax.axis_index("gy"), lax.axis_index("gz")
    x_hi, core = gy // 2, gy % 2
    x, z_hi, z_lo = x_hi * 2 + gz // 4, gz % 4 // 2, gz % 2
    me = y * 16 + x * 4 + z_hi * 2 + core

    def place(y_of, x_of, z_of, core_of):
        return {"gx": y_of, "gy": x_of // 2 * 2 + core_of, "gz": x_of % 2 * 4 + z_of * 2 + 1 - z_lo}

    def peer(j):
        j0, j1, j2 = j % 4, j // 4 % 4, j // 16
        x_of = (x + j0) % 4
        y_of = (y + j0 + j1) % 4
        e = (j0 + j1 + j2) % 4
        z_of, core_of = (z_hi + e) % 2, (core + e // 2) % 2
        return y_of * 16 + x_of * 4 + z_of * 2 + core_of, place(y_of, x_of, z_of, core_of)

    def for_peers(act):
        def one(j, carry):
            act(*peer(j))
            return carry
        lax.fori_loop(0, MEM, one, 0)

    def wait(ref, sem):
        pltpu.make_async_copy(ref, ref, sem).wait()

    stagings = []
    for c in range(PARTS):
        for k, ref in enumerate((tok, grd)):
            copy = pltpu.make_async_copy(ref.at[:, c], staged.at[c, :, :, pl.ds(k * D, D)], stage_sem.at[c, k])
            copy.start()
            stagings.append(copy)

    barrier = pltpu.get_barrier_semaphore()
    for_peers(lambda t, device: pl.semaphore_signal(barrier, inc=1, device_id=device, device_id_type=MESH))
    swap[...] = swap_matrix()
    acc[...] = jnp.zeros_like(acc)
    pl.semaphore_wait(barrier, MEM)

    for c in range(PARTS):
        stagings[2 * c].wait()
        stagings[2 * c + 1].wait()
        for_peers(lambda t, device: pltpu.make_async_remote_copy(
            staged.at[c, t], arrived.at[c, me], go_sem.at[c], come_sem.at[c], device_id=device, device_id_type=MESH).start())

    def part(c, carry):
        wait(arrived.at[c], come_sem.at[c])
        compute_part(arrived.at[c], leaving.at[c], swap[...], wqkv, wout, xw, gw, qkvg, grads, mix, dx, sbuf, pbuf, acc)
        for_peers(lambda t, device: pltpu.make_async_remote_copy(
            leaving.at[c, t], out.at[me, c], back_sem, land_sem, device_id=device, device_id_type=MESH).start())
        return carry

    lax.fori_loop(0, PARTS, part, 0)

    for s in range(MEM):
        accb[s] = acc[s // 4 * 16:s // 4 * 16 + 16, s % 4 * D:s % 4 * D + D].astype(BF)
    for_peers(lambda t, device: pltpu.make_async_remote_copy(
        accb.at[t], terms.at[me], dw_sem.at[0], dw_sem.at[1], device_id=device, device_id_type=MESH).start())
    wait(terms, dw_sem.at[1])
    total = terms[0].astype(F32)
    for s in range(1, MEM):
        total += terms[s].astype(F32)
    half[...] = total
    exchange = pltpu.make_async_remote_copy(
        half, pair, dw_sem.at[2], dw_sem.at[3], device_id=place(y, x, z_hi, core), device_id_type=MESH)
    exchange.start()
    exchange.wait()
    sums[...] = (half[...] + pair[...]).astype(BF)
    for_peers(lambda t, device: pltpu.make_async_remote_copy(
        sums, gathered.at[me], dw_sem.at[4], dw_sem.at[5], device_id=device, device_id_type=MESH).start())
    wait(gathered, dw_sem.at[5])
    for s in range(MEM):
        rows, column = slice(s // 4 * 16, s // 4 * 16 + 16), s % 4
        if column < 3:
            dwqkv[rows, column * D:column * D + D] = gathered[s].astype(F32)
        else:
            dwout[rows, :] = gathered[s].astype(F32)

    for c in range(PARTS):
        wait(staged.at[c], go_sem.at[c])
    wait(leaving, back_sem)
    wait(leaving, land_sem)
    wait(accb, dw_sem.at[0])
    wait(gathered, dw_sem.at[4])


def body(tokens, grad_out, w_qkv, w_out):
    shape = (MEM, PARTS, WIN, D)
    anywhere, vmem = pl.BlockSpec(memory_space=pl.ANY), pl.BlockSpec(memory_space=pltpu.VMEM)
    out, dwqkv, dwout = pl.pallas_call(
        kernel,
        out_shape=(jax.ShapeDtypeStruct(shape, BF), jax.ShapeDtypeStruct((D, 3 * D), F32), jax.ShapeDtypeStruct((D, D), F32)),
        in_specs=[anywhere, anywhere, vmem, vmem],
        out_specs=(anywhere, vmem, vmem),
        scratch_shapes=[
            pltpu.VMEM((PARTS, MEM, WIN, 2 * D), BF),
            pltpu.VMEM((PARTS, MEM, WIN, 2 * D), BF),
            pltpu.VMEM((PARTS, MEM, WIN, D), BF),
            pltpu.VMEM((256, 256), BF),
            pltpu.VMEM((WIN, MEM, D), BF),
            pltpu.VMEM((WIN, MEM, D), BF),
            pltpu.VMEM((WIN, MEM, 4 * D), BF),
            pltpu.VMEM((WIN, MEM, 3 * D), BF),
            pltpu.VMEM((WIN, MEM, D), BF),
            pltpu.VMEM((WIN, MEM, D), BF),
            pltpu.VMEM((2, 2, MEM, 256), F32),
            pltpu.VMEM((2, 2, MEM, 256), BF),
            pltpu.VMEM((D, 4 * D), F32),
            pltpu.VMEM((MEM, 16, D), BF),
            pltpu.VMEM((MEM, 16, D), BF),
            pltpu.VMEM((16, D), F32),
            pltpu.VMEM((16, D), F32),
            pltpu.VMEM((16, D), BF),
            pltpu.VMEM((MEM, 16, D), BF),
            pltpu.SemaphoreType.DMA((PARTS, 2)),
            pltpu.SemaphoreType.DMA((PARTS,)),
            pltpu.SemaphoreType.DMA((PARTS,)),
            pltpu.SemaphoreType.DMA(()),
            pltpu.SemaphoreType.DMA(()),
            pltpu.SemaphoreType.DMA((6,)),
        ],
        compiler_params=pltpu.CompilerParams(collective_id=0, has_side_effects=True, vmem_limit_bytes=48 << 20),
        name="grid_attention_backward",
    )(tokens.reshape(shape), grad_out.reshape(shape), w_qkv, w_out)
    return out.reshape(tokens.shape), dwqkv, dwout


def solution(mesh):
    spec = P("gx", "gy", "gz", None)
    return jax.shard_map(body, mesh=mesh, in_specs=(spec, spec, P(), P()), out_specs=(spec, P(), P()), check_vma=False)
```

```python
import functools
import math

import jax
import jax.numpy as jnp
from jax import lax
from jax.experimental import pallas as pl
from jax.experimental.pallas import tpu as pltpu
from jax.sharding import PartitionSpec as P

BF = jnp.bfloat16
F32 = jnp.float32
LOGICAL = pl.DeviceIdType.LOGICAL
HD = 32
MEM = 64
WIN = 16
PARTS = 4
STEP = 2
CHIPS = 32
D = 256
NN = (((1,), (0,)), ((), ()))
NT = (((1,), (1,)), ((), ()))
TN = (((0,), (0,)), ((), ()))
SCALE = HD ** -0.5


def dot(a, b, dims=NN):
    return lax.dot_general(a, b, dims, preferred_element_type=F32)


def swap_matrix():
    row = lax.broadcasted_iota(jnp.int32, (256, 256), 0)
    col = lax.broadcasted_iota(jnp.int32, (256, 256), 1)
    return jnp.where((row % 16) * 16 + row // 16 == col, 1.0, 0.0).astype(BF)


def spread(rows):
    lane = lax.broadcasted_iota(jnp.int32, (MEM, 128), 1) // HD
    return jnp.concatenate([jnp.where(lane == h, rows, jnp.zeros_like(rows)) for h in range(4)], axis=0)


def gather_heads(wide):
    lane = lax.broadcasted_iota(jnp.int32, (MEM, 128), 1) // HD
    out = wide[3 * MEM:]
    for h in (2, 1, 0):
        out = jnp.where(lane == h, wide[h * MEM:(h + 1) * MEM], out)
    return out


def columns(hg):
    return [slice(b * D + hg * 128, b * D + hg * 128 + 128) for b in range(4)]


def stage1(w, qkvg, sbuf):
    for hg in range(2):
        q, k, v, g = (qkvg[w, :, s] for s in columns(hg))
        sbuf[0, hg] = dot(k, spread(q), NT)
        sbuf[1, hg] = dot(v, spread(g), NT)


def stage2(sbuf, pbuf):
    for hg in range(2):
        scores = sbuf[0, hg]
        top = jnp.max(scores, axis=0, keepdims=True)
        e = jnp.exp2((scores - top) * (SCALE * math.log2(math.e)))
        total = jnp.sum(e, axis=0, keepdims=True)
        att = e * (1.0 / total)
        wg = sbuf[1, hg]
        inner = jnp.sum(att * wg, axis=0, keepdims=True)
        pbuf[hg, :MEM] = att.astype(BF)
        pbuf[hg, MEM:] = (att * ((wg - inner) * SCALE)).astype(BF)


def stage3(w, qkvg, pbuf, mix, grads):
    for hg in range(2):
        s = columns(hg)
        q, k, v, g = (qkvg[w, :, part] for part in s)
        both = pbuf[hg]
        rows = dot(both, jnp.concatenate([spread(g), spread(q)], axis=1))
        grads[w, :, s[2]] = rows[:MEM, :128].astype(BF)
        grads[w, :, s[1]] = rows[MEM:, 128:].astype(BF)
        zero = jnp.zeros_like(v)
        vk = jnp.concatenate([jnp.concatenate([v, zero], axis=1), jnp.concatenate([zero, k], axis=1)], axis=0)
        wide = dot(both, vk, TN)
        mix[w, :, s[0]] = gather_heads(wide[:, :128]).astype(BF)
        grads[w, :, s[0]] = gather_heads(wide[:, 128:]).astype(BF)


def attend(arrived, swap, wqkv, wout, xw, gw, qkvg, grads, mix, sbuf, pbuf, acc):
    for m in range(0, MEM, 16):
        rows = dot(swap[...], arrived[m:m + 16].reshape(256, 512)).astype(BF).reshape(WIN, 16, 512)
        xw[:, m:m + 16, :] = rows[:, :, :D]
        gw[:, m:m + 16, :] = rows[:, :, D:]

    x = xw[...].reshape(-1, D)
    g = gw[...].reshape(-1, D)
    qkvg[:, :, 0:3 * D] = dot(x, wqkv[...]).astype(BF).reshape(WIN, MEM, 3 * D)
    qkvg[:, :, 3 * D:] = dot(g, wout[...], NT).astype(BF).reshape(WIN, MEM, D)

    last = WIN // STEP - 1

    def step(i, carry):
        for u in range(STEP):
            stage3(jnp.maximum(i - 2, 0) * STEP + u, qkvg, pbuf.at[u], mix, grads)
        for u in range(STEP):
            stage2(sbuf.at[u], pbuf.at[u])
        for u in range(STEP):
            stage1(jnp.minimum(i, last) * STEP + u, qkvg, sbuf.at[u])
        return carry

    lax.fori_loop(0, last + 3, step, 0)

    acc[:, 0:3 * D] += dot(xw[...].reshape(-1, D), grads[...].reshape(-1, 3 * D), TN)
    acc[:, 3 * D:] += dot(mix[...].reshape(-1, D), gw[...].reshape(-1, D), TN)


def token_gradients(leaving, swap, wqkv, grads, dx):
    dx[...] = dot(grads[...].reshape(-1, 3 * D), wqkv[...], NT).astype(BF).reshape(WIN, MEM, D)
    for m in range(0, MEM, 16):
        rows = dx[:, m:m + 16, :].reshape(256, D)
        leaving[m:m + 16] = dot(swap[...], rows).astype(BF).reshape(16, WIN, D)


def kernel(tok, grd, wqkv_hbm, wout_hbm, out, dwqkv, dwout, staged, arrived, leaving, wqkv, wout, swap, xw, gw, qkvg, grads,
           mix, dx, sbuf, pbuf, acc, away, home, terms, half, pair, gathered,
           stage_sem, weight_sem, go_sem, come_sem, back_sem, land_sem, dw_sem):
    y, gy, gz = lax.axis_index("gx"), lax.axis_index("gy"), lax.axis_index("gz")
    x_hi, core = gy // 2, gy % 2
    x, z_hi, z_lo = x_hi * 2 + gz // 4, gz % 4 // 2, gz % 2
    chip = y * 8 + x * 2 + z_hi
    me = chip * 2 + core

    def device(y_of, x_of, z_of, core_of, z_low):
        return y_of * 32 + x_of // 2 * 16 + core_of * 8 + x_of % 2 * 4 + z_of * 2 + z_low

    ys = tuple((y + d) % 4 for d in range(4))
    xs = tuple((x + d) % 4 for d in range(4))
    ends = tuple(((z_hi + e) % 2, (core + e // 2) % 2) for e in range(4))
    y_part = tuple(v * 16 for v in ys)
    x_part = tuple((v * 4, device(0, v, 0, 0, 1 - z_lo)) for v in xs)
    end_part = tuple((z_of * 2 + core_of, device(0, 0, z_of, core_of, 0)) for z_of, core_of in ends)

    def for_partners(act):
        def outer(i, y_carry):
            def inner(k, e_carry):
                for d in range(4):
                    y_of, (x_num, x_dev), (e_num, e_dev) = y_carry[d], x_part[d], e_carry[d]
                    act(y_of + x_num + e_num, y_of * 2 + x_dev + e_dev)
                return e_carry[1:] + e_carry[:1]
            lax.fori_loop(0, 4, inner, end_part)
            return y_carry[1:] + y_carry[:1]
        lax.fori_loop(0, 4, outer, y_part)

    def for_chips(act):
        def outer(i, y_carry):
            for d in range(4):
                for z_of in (z_hi, 1 - z_hi):
                    y_of, (x_num, x_dev) = y_carry[d], x_part[d]
                    act((y_of + x_num) // 2 + z_of, y_of * 2 + x_dev + device(0, 0, z_of, core, 0))
            return y_carry[1:] + y_carry[:1]
        lax.fori_loop(0, 4, outer, y_part)

    other_core = device(y, x, z_hi, 1 - core, z_lo)
    across = device(y, x, z_hi, core, 1 - z_lo)

    def send(src, dst, send_sem, recv_sem, to):
        copy = pltpu.make_async_remote_copy(src, dst, send_sem, recv_sem, device_id=to, device_id_type=LOGICAL)
        copy.start()
        return copy

    def wait(ref, sem):
        pltpu.make_async_copy(ref, ref, sem).wait()

    stagings = []
    for c in range(PARTS):
        for k, ref in enumerate((tok, grd)):
            copy = pltpu.make_async_copy(ref.at[:, c], staged.at[c, :, :, pl.ds(k * D, D)], stage_sem.at[c, k])
            copy.start()
            stagings.append(copy)
    weights = [pltpu.make_async_copy(wqkv_hbm, wqkv, weight_sem.at[0]), pltpu.make_async_copy(wout_hbm, wout, weight_sem.at[1])]
    for copy in weights:
        copy.start()

    barrier = pltpu.get_barrier_semaphore()
    for_partners(lambda t, to: pl.semaphore_signal(barrier, inc=1, device_id=to, device_id_type=LOGICAL))
    pl.semaphore_signal(barrier, inc=1, device_id=other_core, device_id_type=LOGICAL)
    swap[...] = swap_matrix()
    acc[...] = jnp.zeros_like(acc)
    pl.semaphore_wait(barrier, MEM + 1)

    for c in range(PARTS):
        stagings[2 * c].wait()
        stagings[2 * c + 1].wait()
        for_partners(lambda t, to: send(staged.at[c, t], arrived.at[c, me], go_sem.at[c], come_sem.at[c], to))
    for copy in weights:
        copy.wait()

    rows = D // 2
    first, second = pl.ds(pl.multiple_of(core * rows, rows), rows), pl.ds(pl.multiple_of((1 - core) * rows, rows), rows)

    def part(c, carry):
        wait(arrived.at[c], come_sem.at[c])
        attend(arrived.at[c], swap, wqkv, wout, xw, gw, qkvg, grads, mix, sbuf, pbuf, acc)

        @pl.when(c == PARTS - 1)
        def _():
            away[0] = acc[second, :].astype(BF)
            send(away.at[0], away.at[1], dw_sem.at[0], dw_sem.at[1], other_core)

        token_gradients(leaving.at[c], swap, wqkv, grads, dx)

        @pl.when(c == PARTS - 1)
        def _():
            wait(away.at[1], dw_sem.at[1])
            both = (acc[first, :] + away[1].astype(F32)).astype(BF)
            for s in range(CHIPS):
                home[s] = both[s // 4 * 16:s // 4 * 16 + 16, s % 4 * D:s % 4 * D + D]
            for_chips(lambda t, to: send(home.at[t], terms.at[chip], dw_sem.at[2], dw_sem.at[3], to))

        for_partners(lambda t, to: send(leaving.at[c, t], out.at[me, c], back_sem, land_sem, to))
        return carry

    lax.fori_loop(0, PARTS, part, 0)

    wait(terms, dw_sem.at[3])
    total = terms[0].astype(F32)
    for s in range(1, CHIPS):
        total += terms[s].astype(F32)
    half[...] = total
    send(half, pair, dw_sem.at[4], dw_sem.at[5], across).wait()
    mine = home.at[CHIPS]
    mine[...] = (half[...] + pair[...]).astype(BF)
    for_chips(lambda t, to: send(mine, gathered.at[0, chip], dw_sem.at[6], dw_sem.at[7], to))
    wait(gathered.at[0], dw_sem.at[7])
    send(gathered.at[0], gathered.at[1], dw_sem.at[8], dw_sem.at[9], other_core)

    def write(owner, block):
        for s in range(CHIPS):
            where = pl.ds(pl.multiple_of(owner * rows + s // 4 * 16, 16), 16)
            if s % 4 < 3:
                dwqkv[where, s % 4 * D:s % 4 * D + D] = block[s].astype(F32)
            else:
                dwout[where, :] = block[s].astype(F32)

    write(core, gathered.at[0])
    wait(gathered.at[1], dw_sem.at[9])
    write(1 - core, gathered.at[1])

    for c in range(PARTS):
        wait(staged.at[c], go_sem.at[c])
    wait(leaving, back_sem)
    wait(leaving, land_sem)
    wait(away.at[0], dw_sem.at[0])
    wait(terms, dw_sem.at[2])
    wait(gathered.at[0], dw_sem.at[6])
    wait(gathered.at[0], dw_sem.at[8])


def body(tokens, grad_out, w_qkv, w_out):
    shape = (MEM, PARTS, WIN, D)
    hbm, anywhere, vmem = (pl.BlockSpec(memory_space=space) for space in (pltpu.HBM, pl.ANY, pltpu.VMEM))
    out, dwqkv, dwout = pl.pallas_call(
        kernel,
        out_shape=(jax.ShapeDtypeStruct(shape, BF), jax.ShapeDtypeStruct((D, 3 * D), F32), jax.ShapeDtypeStruct((D, D), F32)),
        in_specs=[hbm, hbm, hbm, hbm],
        out_specs=(anywhere, vmem, vmem),
        scratch_shapes=[
            pltpu.VMEM((PARTS, MEM, WIN, 2 * D), BF),
            pltpu.VMEM((PARTS, MEM, WIN, 2 * D), BF),
            pltpu.VMEM((PARTS, MEM, WIN, D), BF),
            pltpu.VMEM((D, 3 * D), BF),
            pltpu.VMEM((D, D), BF),
            pltpu.VMEM((256, 256), BF),
            pltpu.VMEM((WIN, MEM, D), BF),
            pltpu.VMEM((WIN, MEM, D), BF),
            pltpu.VMEM((WIN, MEM, 4 * D), BF),
            pltpu.VMEM((WIN, MEM, 3 * D), BF),
            pltpu.VMEM((WIN, MEM, D), BF),
            pltpu.VMEM((WIN, MEM, D), BF),
            pltpu.VMEM((STEP, 2, 2, MEM, 256), F32),
            pltpu.VMEM((STEP, 2, 2 * MEM, 256), BF),
            pltpu.VMEM((D, 4 * D), F32),
            pltpu.VMEM((2, D // 2, 4 * D), BF),
            pltpu.VMEM((CHIPS + 1, 16, D), BF),
            pltpu.VMEM((CHIPS, 16, D), BF),
            pltpu.VMEM((16, D), F32),
            pltpu.VMEM((16, D), F32),
            pltpu.VMEM((2, CHIPS, 16, D), BF),
            pltpu.SemaphoreType.DMA((PARTS, 2)),
            pltpu.SemaphoreType.DMA((2,)),
            pltpu.SemaphoreType.DMA((PARTS,)),
            pltpu.SemaphoreType.DMA((PARTS,)),
            pltpu.SemaphoreType.DMA(()),
            pltpu.SemaphoreType.DMA(()),
            pltpu.SemaphoreType.DMA((10,)),
        ],
        compiler_params=pltpu.CompilerParams(collective_id=0, has_side_effects=True, vmem_limit_bytes=48 << 20),
        name="grid_attention_backward",
    )(*(pltpu.with_memory_space_constraint(a, pltpu.HBM) for a in (tokens.reshape(shape), grad_out.reshape(shape), w_qkv, w_out)))
    return out.reshape(tokens.shape), dwqkv, dwout


def solution(mesh):
    spec = P("gx", "gy", "gz", None)
    return jax.shard_map(body, mesh=mesh, in_specs=(spec, spec, P(), P()), out_specs=(spec, P(), P()), check_vma=False)
```

```python
import functools
import math

import jax
import jax.numpy as jnp
from jax import lax
from jax.experimental import pallas as pl
from jax.experimental.pallas import tpu as pltpu
from jax.sharding import PartitionSpec as P

BF = jnp.bfloat16
F32 = jnp.float32
LOGICAL = pl.DeviceIdType.LOGICAL
HD = 32
MEM = 64
WIN = 16
PARTS = 4
STEP = 2
CHIPS = 32
D = 256
NN = (((1,), (0,)), ((), ()))
NT = (((1,), (1,)), ((), ()))
TN = (((0,), (0,)), ((), ()))
SCALE = HD ** -0.5


def dot(a, b, dims=NN):
    return lax.dot_general(a, b, dims, preferred_element_type=F32)


def swap_matrix():
    row = lax.broadcasted_iota(jnp.int32, (256, 256), 0)
    col = lax.broadcasted_iota(jnp.int32, (256, 256), 1)
    return jnp.where((row % 16) * 16 + row // 16 == col, 1.0, 0.0).astype(BF)


def spread(rows):
    lane = lax.broadcasted_iota(jnp.int32, (MEM, 128), 1) // HD
    return jnp.concatenate([jnp.where(lane == h, rows, jnp.zeros_like(rows)) for h in range(4)], axis=0)


def gather_heads(wide):
    lane = lax.broadcasted_iota(jnp.int32, (MEM, 128), 1) // HD
    out = wide[3 * MEM:]
    for h in (2, 1, 0):
        out = jnp.where(lane == h, wide[h * MEM:(h + 1) * MEM], out)
    return out


def columns(hg):
    return [slice(b * D + hg * 128, b * D + hg * 128 + 128) for b in range(4)]


def stage1(w, qkvg, sbuf):
    for hg in range(2):
        q, k, v, g = (qkvg[w, :, s] for s in columns(hg))
        sbuf[0, hg] = dot(k, spread(q), NT)
        sbuf[1, hg] = dot(v, spread(g), NT)


def stage2(sbuf, pbuf):
    for hg in range(2):
        scores = sbuf[0, hg]
        top = jnp.max(scores, axis=0, keepdims=True)
        e = jnp.exp2((scores - top) * (SCALE * math.log2(math.e)))
        total = jnp.sum(e, axis=0, keepdims=True)
        att = e * (1.0 / total)
        wg = sbuf[1, hg]
        inner = jnp.sum(att * wg, axis=0, keepdims=True)
        pbuf[hg, :MEM] = att.astype(BF)
        pbuf[hg, MEM:] = (att * ((wg - inner) * SCALE)).astype(BF)


def stage3(w, qkvg, pbuf, mix, grads):
    for hg in range(2):
        s = columns(hg)
        q, k, v, g = (qkvg[w, :, part] for part in s)
        both = pbuf[hg]
        rows = dot(both, jnp.concatenate([spread(g), spread(q)], axis=1))
        grads[w, :, s[2]] = rows[:MEM, :128].astype(BF)
        grads[w, :, s[1]] = rows[MEM:, 128:].astype(BF)
        zero = jnp.zeros_like(v)
        vk = jnp.concatenate([jnp.concatenate([v, zero], axis=1), jnp.concatenate([zero, k], axis=1)], axis=0)
        wide = dot(both, vk, TN)
        mix[w, :, s[0]] = gather_heads(wide[:, :128]).astype(BF)
        grads[w, :, s[0]] = gather_heads(wide[:, 128:]).astype(BF)


def attend(arrived, swap, wqkv, wout, xw, gw, qkvg, grads, mix, sbuf, pbuf, acc):
    for m in range(0, MEM, 16):
        rows = dot(swap[...], arrived[m:m + 16].reshape(256, 512)).astype(BF).reshape(WIN, 16, 512)
        xw[:, m:m + 16, :] = rows[:, :, :D]
        gw[:, m:m + 16, :] = rows[:, :, D:]

    x = xw[...].reshape(-1, D)
    g = gw[...].reshape(-1, D)
    qkvg[:, :, 0:3 * D] = dot(x, wqkv[...]).astype(BF).reshape(WIN, MEM, 3 * D)
    qkvg[:, :, 3 * D:] = dot(g, wout[...], NT).astype(BF).reshape(WIN, MEM, D)

    last = WIN // STEP - 1

    def step(i, carry):
        for u in range(STEP):
            stage3(jnp.maximum(i - 2, 0) * STEP + u, qkvg, pbuf.at[u], mix, grads)
        for u in range(STEP):
            stage2(sbuf.at[u], pbuf.at[u])
        for u in range(STEP):
            stage1(jnp.minimum(i, last) * STEP + u, qkvg, sbuf.at[u])
        return carry

    lax.fori_loop(0, last + 3, step, 0)

    acc[:, 0:3 * D] += dot(xw[...].reshape(-1, D), grads[...].reshape(-1, 3 * D), TN)
    acc[:, 3 * D:] += dot(mix[...].reshape(-1, D), gw[...].reshape(-1, D), TN)


def token_gradients(leaving, swap, wqkv, grads, dx):
    dx[...] = dot(grads[...].reshape(-1, 3 * D), wqkv[...], NT).astype(BF).reshape(WIN, MEM, D)
    for m in range(0, MEM, 16):
        rows = dx[:, m:m + 16, :].reshape(256, D)
        leaving[m:m + 16] = dot(swap[...], rows).astype(BF).reshape(16, WIN, D)


def kernel(tok, grd, wqkv_hbm, wout_hbm, out, dwqkv, dwout, staged, arrived, leaving, wqkv, wout, swap, xw, gw, qkvg, grads,
           mix, dx, sbuf, pbuf, acc, away, home, terms, half, pair, gathered,
           stage_sem, weight_sem, go_sem, come_sem, back_sem, land_sem, dw_sem):
    y, gy, gz = lax.axis_index("gx"), lax.axis_index("gy"), lax.axis_index("gz")
    x_hi, core = gy // 2, gy % 2
    x, z_hi, z_lo = x_hi * 2 + gz // 4, gz % 4 // 2, gz % 2
    chip = y * 8 + x * 2 + z_hi
    me = chip * 2 + core

    def device(y_of, x_of, z_of, core_of, z_low):
        return y_of * 32 + x_of // 2 * 16 + core_of * 8 + x_of % 2 * 4 + z_of * 2 + z_low

    ys = tuple((y + d) % 4 for d in range(4))
    xs = tuple((x + d) % 4 for d in range(4))
    ends = tuple(((z_hi + e) % 2, (core + e // 2) % 2) for e in range(4))
    y_part = tuple(v * 16 for v in ys)
    x_part = tuple((v * 4, device(0, v, 0, 0, 1 - z_lo)) for v in xs)
    end_part = tuple((z_of * 2 + core_of, device(0, 0, z_of, core_of, 0)) for z_of, core_of in ends)

    def for_partners(act, first=0, last=4):
        def outer(i, y_carry):
            def inner(k, e_carry):
                for d in range(4):
                    y_of, (x_num, x_dev), (e_num, e_dev) = y_carry[d], x_part[d], e_carry[d]
                    act(y_of + x_num + e_num, y_of * 2 + x_dev + e_dev)
                return e_carry[1:] + e_carry[:1]
            lax.fori_loop(0, 4, inner, end_part)
            return y_carry[1:] + y_carry[:1]
        lax.fori_loop(first, last, outer, y_part[first:] + y_part[:first])

    def for_chips(act):
        def outer(i, y_carry):
            for d in range(4):
                for z_of in (z_hi, 1 - z_hi):
                    y_of, (x_num, x_dev) = y_carry[d], x_part[d]
                    act((y_of + x_num) // 2 + z_of, y_of * 2 + x_dev + device(0, 0, z_of, core, 0))
            return y_carry[1:] + y_carry[:1]
        lax.fori_loop(0, 4, outer, y_part)

    other_core = device(y, x, z_hi, 1 - core, z_lo)
    across = device(y, x, z_hi, core, 1 - z_lo)

    def send(src, dst, send_sem, recv_sem, to):
        copy = pltpu.make_async_remote_copy(src, dst, send_sem, recv_sem, device_id=to, device_id_type=LOGICAL)
        copy.start()
        return copy

    def wait(ref, sem):
        pltpu.make_async_copy(ref, ref, sem).wait()

    barrier = pltpu.get_barrier_semaphore()
    for_partners(lambda t, to: pl.semaphore_signal(barrier, inc=1, device_id=to, device_id_type=LOGICAL))
    pl.semaphore_signal(barrier, inc=1, device_id=other_core, device_id_type=LOGICAL)
    stagings = []
    for c in range(PARTS):
        for k, ref in enumerate((tok, grd)):
            copy = pltpu.make_async_copy(ref.at[:, c], staged.at[c, :, :, pl.ds(k * D, D)], stage_sem.at[c, k])
            copy.start()
            stagings.append(copy)
    weights = [pltpu.make_async_copy(wqkv_hbm, wqkv, weight_sem.at[0]), pltpu.make_async_copy(wout_hbm, wout, weight_sem.at[1])]
    for copy in weights:
        copy.start()

    swap[...] = swap_matrix()
    acc[...] = jnp.zeros_like(acc)
    pl.semaphore_wait(barrier, MEM + 1)

    for c in range(PARTS):
        stagings[2 * c].wait()
        stagings[2 * c + 1].wait()
        for_partners(lambda t, to: send(staged.at[c, t], arrived.at[c, me], go_sem.at[c], come_sem.at[c], to))
    for copy in weights:
        copy.wait()

    def send_back(c, first=0, last=4):
        for_partners(lambda t, to: send(leaving.at[c, t], out.at[me, c], back_sem, land_sem, to), first, last)

    rows = D // 2
    first, second = pl.ds(pl.multiple_of(core * rows, rows), rows), pl.ds(pl.multiple_of((1 - core) * rows, rows), rows)

    def part(c, carry):
        wait(arrived.at[c], come_sem.at[c])
        attend(arrived.at[c], swap, wqkv, wout, xw, gw, qkvg, grads, mix, sbuf, pbuf, acc)

        @pl.when(c == PARTS - 1)
        def _():
            away[0] = acc[second, :].astype(BF)
            send(away.at[0], away.at[1], dw_sem.at[0], dw_sem.at[1], other_core)

        token_gradients(leaving.at[c], swap, wqkv, grads, dx)

        @pl.when(c == PARTS - 1)
        def _():
            wait(away.at[1], dw_sem.at[1])
            both = (acc[first, :] + away[1].astype(F32)).astype(BF)
            for s in range(CHIPS):
                home[s] = both[s // 4 * 16:s // 4 * 16 + 16, s % 4 * D:s % 4 * D + D]
            for_chips(lambda t, to: send(home.at[t], terms.at[chip], dw_sem.at[2], dw_sem.at[3], to))
            send_back(2, 2, 4)
            send_back(3, 0, 1)

        @pl.when(c == 0)
        def _():
            send_back(0, 0, 4)

        @pl.when(c == 1)
        def _():
            send_back(1, 0, 3)

        @pl.when(c == 2)
        def _():
            send_back(1, 3, 4)
            send_back(2, 0, 2)

        return carry

    lax.fori_loop(0, PARTS, part, 0)

    wait(terms, dw_sem.at[3])
    total = terms[0].astype(F32)
    for s in range(1, CHIPS):
        total += terms[s].astype(F32)
    half[...] = total
    exchange = send(half, pair, dw_sem.at[4], dw_sem.at[5], across)
    send_back(3, 1, 2)
    exchange.wait()
    mine = home.at[CHIPS]
    mine[...] = (half[...] + pair[...]).astype(BF)
    for_chips(lambda t, to: send(mine, gathered.at[0, chip], dw_sem.at[6], dw_sem.at[7], to))
    send_back(3, 2, 4)
    wait(gathered.at[0], dw_sem.at[7])
    send(gathered.at[0], gathered.at[1], dw_sem.at[8], dw_sem.at[9], other_core)

    def write(owner, block):
        for s in range(CHIPS):
            where = pl.ds(pl.multiple_of(owner * rows + s // 4 * 16, 16), 16)
            if s % 4 < 3:
                dwqkv[where, s % 4 * D:s % 4 * D + D] = block[s].astype(F32)
            else:
                dwout[where, :] = block[s].astype(F32)

    write(core, gathered.at[0])
    wait(gathered.at[1], dw_sem.at[9])
    write(1 - core, gathered.at[1])

    for c in range(PARTS):
        wait(staged.at[c], go_sem.at[c])
    wait(leaving, back_sem)
    wait(leaving, land_sem)
    wait(away.at[0], dw_sem.at[0])
    wait(terms, dw_sem.at[2])
    wait(gathered.at[0], dw_sem.at[6])
    wait(gathered.at[0], dw_sem.at[8])


def body(tokens, grad_out, w_qkv, w_out):
    shape = (MEM, PARTS, WIN, D)
    hbm, anywhere, vmem = (pl.BlockSpec(memory_space=space) for space in (pltpu.HBM, pl.ANY, pltpu.VMEM))
    out, dwqkv, dwout = pl.pallas_call(
        kernel,
        out_shape=(jax.ShapeDtypeStruct(shape, BF), jax.ShapeDtypeStruct((D, 3 * D), F32), jax.ShapeDtypeStruct((D, D), F32)),
        in_specs=[hbm, hbm, hbm, hbm],
        out_specs=(anywhere, vmem, vmem),
        scratch_shapes=[
            pltpu.VMEM((PARTS, MEM, WIN, 2 * D), BF),
            pltpu.VMEM((PARTS, MEM, WIN, 2 * D), BF),
            pltpu.VMEM((PARTS, MEM, WIN, D), BF),
            pltpu.VMEM((D, 3 * D), BF),
            pltpu.VMEM((D, D), BF),
            pltpu.VMEM((256, 256), BF),
            pltpu.VMEM((WIN, MEM, D), BF),
            pltpu.VMEM((WIN, MEM, D), BF),
            pltpu.VMEM((WIN, MEM, 4 * D), BF),
            pltpu.VMEM((WIN, MEM, 3 * D), BF),
            pltpu.VMEM((WIN, MEM, D), BF),
            pltpu.VMEM((WIN, MEM, D), BF),
            pltpu.VMEM((STEP, 2, 2, MEM, 256), F32),
            pltpu.VMEM((STEP, 2, 2 * MEM, 256), BF),
            pltpu.VMEM((D, 4 * D), F32),
            pltpu.VMEM((2, D // 2, 4 * D), BF),
            pltpu.VMEM((CHIPS + 1, 16, D), BF),
            pltpu.VMEM((CHIPS, 16, D), BF),
            pltpu.VMEM((16, D), F32),
            pltpu.VMEM((16, D), F32),
            pltpu.VMEM((2, CHIPS, 16, D), BF),
            pltpu.SemaphoreType.DMA((PARTS, 2)),
            pltpu.SemaphoreType.DMA((2,)),
            pltpu.SemaphoreType.DMA((PARTS,)),
            pltpu.SemaphoreType.DMA((PARTS,)),
            pltpu.SemaphoreType.DMA(()),
            pltpu.SemaphoreType.DMA(()),
            pltpu.SemaphoreType.DMA((10,)),
        ],
        compiler_params=pltpu.CompilerParams(collective_id=0, has_side_effects=True, vmem_limit_bytes=48 << 20),
        name="grid_attention_backward",
    )(*(pltpu.with_memory_space_constraint(a, pltpu.HBM) for a in (tokens.reshape(shape), grad_out.reshape(shape), w_qkv, w_out)))
    return out.reshape(tokens.shape), dwqkv, dwout


def solution(mesh):
    spec = P("gx", "gy", "gz", None)
    return jax.shard_map(body, mesh=mesh, in_specs=(spec, spec, P(), P()), out_specs=(spec, P(), P()), check_vma=False)
```

```python
import functools
import math

import jax
import jax.numpy as jnp
from jax import lax
from jax.experimental import pallas as pl
from jax.experimental.pallas import tpu as pltpu
from jax.sharding import PartitionSpec as P

BF = jnp.bfloat16
F32 = jnp.float32
LOGICAL = pl.DeviceIdType.LOGICAL
HD = 32
MEM = 64
WIN = 16
PARTS = 4
STEP = 2
CHIPS = 32
D = 256
NN = (((1,), (0,)), ((), ()))
NT = (((1,), (1,)), ((), ()))
TN = (((0,), (0,)), ((), ()))
SCALE = HD ** -0.5


def dot(a, b, dims=NN):
    return lax.dot_general(a, b, dims, preferred_element_type=F32)


def swap_matrix():
    row = lax.broadcasted_iota(jnp.int32, (256, 256), 0)
    col = lax.broadcasted_iota(jnp.int32, (256, 256), 1)
    return jnp.where((row % 16) * 16 + row // 16 == col, 1.0, 0.0).astype(BF)


def spread(rows):
    lane = lax.broadcasted_iota(jnp.int32, (MEM, 128), 1) // HD
    return jnp.concatenate([jnp.where(lane == h, rows, jnp.zeros_like(rows)) for h in range(4)], axis=0)


def gather_heads(wide):
    lane = lax.broadcasted_iota(jnp.int32, (MEM, 128), 1) // HD
    out = wide[3 * MEM:]
    for h in (2, 1, 0):
        out = jnp.where(lane == h, wide[h * MEM:(h + 1) * MEM], out)
    return out


def columns(hg):
    return [slice(b * D + hg * 128, b * D + hg * 128 + 128) for b in range(4)]


def stage1(w, qkvg, sbuf):
    for hg in range(2):
        q, k, v, g = (qkvg[w, :, s] for s in columns(hg))
        sbuf[0, hg] = dot(k, spread(q), NT)
        sbuf[1, hg] = dot(v, spread(g), NT)


def stage2(sbuf, pbuf):
    for hg in range(2):
        scores = sbuf[0, hg]
        top = jnp.max(scores, axis=0, keepdims=True)
        e = jnp.exp2((scores - top) * (SCALE * math.log2(math.e)))
        total = jnp.sum(e, axis=0, keepdims=True)
        att = e * (1.0 / total)
        wg = sbuf[1, hg]
        inner = jnp.sum(att * wg, axis=0, keepdims=True)
        pbuf[hg, :MEM] = att.astype(BF)
        pbuf[hg, MEM:] = (att * ((wg - inner) * SCALE)).astype(BF)


def stage3(w, qkvg, pbuf, mix, grads):
    for hg in range(2):
        s = columns(hg)
        q, k, v, g = (qkvg[w, :, part] for part in s)
        both = pbuf[hg]
        rows = dot(both, jnp.concatenate([spread(g), spread(q)], axis=1))
        grads[w, :, s[2]] = rows[:MEM, :128].astype(BF)
        grads[w, :, s[1]] = rows[MEM:, 128:].astype(BF)
        zero = jnp.zeros_like(v)
        vk = jnp.concatenate([jnp.concatenate([v, zero], axis=1), jnp.concatenate([zero, k], axis=1)], axis=0)
        wide = dot(both, vk, TN)
        mix[w, :, s[0]] = gather_heads(wide[:, :128]).astype(BF)
        grads[w, :, s[0]] = gather_heads(wide[:, 128:]).astype(BF)


def attend(arrived, swap, wqkv, wout, xw, gw, qkvg, grads, mix, sbuf, pbuf, acc):
    for m in range(0, MEM, 16):
        rows = dot(swap[...], arrived[m:m + 16].reshape(256, 512)).astype(BF).reshape(WIN, 16, 512)
        xw[:, m:m + 16, :] = rows[:, :, :D]
        gw[:, m:m + 16, :] = rows[:, :, D:]

    x = xw[...].reshape(-1, D)
    g = gw[...].reshape(-1, D)
    qkvg[:, :, 0:3 * D] = dot(x, wqkv[...]).astype(BF).reshape(WIN, MEM, 3 * D)
    qkvg[:, :, 3 * D:] = dot(g, wout[...], NT).astype(BF).reshape(WIN, MEM, D)

    last = WIN // STEP - 1

    def step(i, carry):
        for u in range(STEP):
            stage3(jnp.maximum(i - 2, 0) * STEP + u, qkvg, pbuf.at[u], mix, grads)
        for u in range(STEP):
            stage2(sbuf.at[u], pbuf.at[u])
        for u in range(STEP):
            stage1(jnp.minimum(i, last) * STEP + u, qkvg, sbuf.at[u])
        return carry

    lax.fori_loop(0, last + 3, step, 0)

    acc[:, 0:3 * D] += dot(xw[...].reshape(-1, D), grads[...].reshape(-1, 3 * D), TN)
    acc[:, 3 * D:] += dot(mix[...].reshape(-1, D), gw[...].reshape(-1, D), TN)


def token_gradients(leaving, swap, wqkv, grads, dx):
    dx[...] = dot(grads[...].reshape(-1, 3 * D), wqkv[...], NT).astype(BF).reshape(WIN, MEM, D)
    for m in range(0, MEM, 16):
        rows = dx[:, m:m + 16, :].reshape(256, D)
        leaving[m:m + 16] = dot(swap[...], rows).astype(BF).reshape(16, WIN, D)


def kernel(tok, grd, wqkv_hbm, wout_hbm, out, dwqkv, dwout, staged, arrived, leaving, wqkv, wout, swap, xw, gw, qkvg, grads,
           mix, dx, sbuf, pbuf, acc, away, home, terms, half, pair, gathered,
           stage_sem, weight_sem, go_sem, come_sem, back_sem, land_sem, dw_sem):
    y, gy, gz = lax.axis_index("gx"), lax.axis_index("gy"), lax.axis_index("gz")
    x_hi, core = gy // 2, gy % 2
    x, z_hi, z_lo = x_hi * 2 + gz // 4, gz % 4 // 2, gz % 2
    chip = y * 8 + x * 2 + z_hi
    me = chip * 2 + core

    def device(y_of, x_of, z_of, core_of, z_low):
        return y_of * 32 + x_of // 2 * 16 + core_of * 8 + x_of % 2 * 4 + z_of * 2 + z_low

    ys = tuple((y + d) % 4 for d in range(4))
    xs = tuple((x + d) % 4 for d in range(4))
    ends = tuple(((z_hi + e) % 2, (core + e // 2) % 2) for e in range(4))
    y_part = tuple(v * 16 for v in ys)
    x_part = tuple((v * 4, device(0, v, 0, 0, 1 - z_lo)) for v in xs)
    end_part = tuple((z_of * 2 + core_of, device(0, 0, z_of, core_of, 0)) for z_of, core_of in ends)

    def for_partners(act, first=0, last=4):
        def outer(k, e_carry):
            def inner(i, carry):
                y_carry, e_now = carry
                for d in range(4):
                    y_of, (x_num, x_dev), (e_num, e_dev) = y_carry[d], x_part[d], e_now[d]
                    act(y_of + x_num + e_num, y_of * 2 + x_dev + e_dev)
                return y_carry[1:] + y_carry[:1], e_now[-1:] + e_now[:-1]
            lax.fori_loop(0, 4, inner, (y_part, e_carry))
            return e_carry[1:] + e_carry[:1]
        lax.fori_loop(first, last, outer, end_part[first:] + end_part[:first])

    def for_chips(act):
        def outer(i, y_carry):
            for d in range(4):
                for z_of in (z_hi, 1 - z_hi):
                    y_of, (x_num, x_dev) = y_carry[d], x_part[d]
                    act((y_of + x_num) // 2 + z_of, y_of * 2 + x_dev + device(0, 0, z_of, core, 0))
            return y_carry[1:] + y_carry[:1]
        lax.fori_loop(0, 4, outer, y_part)

    other_core = device(y, x, z_hi, 1 - core, z_lo)
    across = device(y, x, z_hi, core, 1 - z_lo)

    def send(src, dst, send_sem, recv_sem, to):
        copy = pltpu.make_async_remote_copy(src, dst, send_sem, recv_sem, device_id=to, device_id_type=LOGICAL)
        copy.start()
        return copy

    def wait(ref, sem):
        pltpu.make_async_copy(ref, ref, sem).wait()

    barrier = pltpu.get_barrier_semaphore()
    for_partners(lambda t, to: pl.semaphore_signal(barrier, inc=1, device_id=to, device_id_type=LOGICAL))
    pl.semaphore_signal(barrier, inc=1, device_id=other_core, device_id_type=LOGICAL)
    stagings = []
    for c in range(PARTS):
        for k, ref in enumerate((tok, grd)):
            copy = pltpu.make_async_copy(ref.at[:, c], staged.at[c, :, :, pl.ds(k * D, D)], stage_sem.at[c, k])
            copy.start()
            stagings.append(copy)
    weights = [pltpu.make_async_copy(wqkv_hbm, wqkv, weight_sem.at[0]), pltpu.make_async_copy(wout_hbm, wout, weight_sem.at[1])]
    for copy in weights:
        copy.start()

    swap[...] = swap_matrix()
    acc[...] = jnp.zeros_like(acc)
    pl.semaphore_wait(barrier, MEM + 1)

    for c in range(PARTS):
        stagings[2 * c].wait()
        stagings[2 * c + 1].wait()
        for_partners(lambda t, to: send(staged.at[c, t], arrived.at[c, me], go_sem.at[c], come_sem.at[c], to))
    for copy in weights:
        copy.wait()

    def send_back(c, first=0, last=4):
        for_partners(lambda t, to: send(leaving.at[c, t], out.at[me, c], back_sem, land_sem, to), first, last)

    rows = D // 2
    first, second = pl.ds(pl.multiple_of(core * rows, rows), rows), pl.ds(pl.multiple_of((1 - core) * rows, rows), rows)

    def part(c, carry):
        wait(arrived.at[c], come_sem.at[c])
        attend(arrived.at[c], swap, wqkv, wout, xw, gw, qkvg, grads, mix, sbuf, pbuf, acc)

        @pl.when(c == PARTS - 1)
        def _():
            away[0] = acc[second, :].astype(BF)
            send(away.at[0], away.at[1], dw_sem.at[0], dw_sem.at[1], other_core)

        token_gradients(leaving.at[c], swap, wqkv, grads, dx)

        @pl.when(c == PARTS - 1)
        def _():
            wait(away.at[1], dw_sem.at[1])
            both = (acc[first, :] + away[1].astype(F32)).astype(BF)
            for s in range(CHIPS):
                home[s] = both[s // 4 * 16:s // 4 * 16 + 16, s % 4 * D:s % 4 * D + D]
            for_chips(lambda t, to: send(home.at[t], terms.at[chip], dw_sem.at[2], dw_sem.at[3], to))
            send_back(2, 2, 4)
            send_back(3, 0, 1)

        @pl.when(c == 0)
        def _():
            send_back(0, 0, 4)

        @pl.when(c == 1)
        def _():
            send_back(1, 0, 3)

        @pl.when(c == 2)
        def _():
            send_back(1, 3, 4)
            send_back(2, 0, 2)

        return carry

    lax.fori_loop(0, PARTS, part, 0)

    wait(terms, dw_sem.at[3])
    total = terms[0].astype(F32)
    for s in range(1, CHIPS):
        total += terms[s].astype(F32)
    half[...] = total
    exchange = send(half, pair, dw_sem.at[4], dw_sem.at[5], across)
    send_back(3, 1, 2)
    exchange.wait()
    mine = home.at[CHIPS]
    mine[...] = (half[...] + pair[...]).astype(BF)
    for_chips(lambda t, to: send(mine, gathered.at[0, chip], dw_sem.at[6], dw_sem.at[7], to))
    send_back(3, 2, 4)
    wait(gathered.at[0], dw_sem.at[7])
    send(gathered.at[0], gathered.at[1], dw_sem.at[8], dw_sem.at[9], other_core)

    def write(owner, block):
        for s in range(CHIPS):
            where = pl.ds(pl.multiple_of(owner * rows + s // 4 * 16, 16), 16)
            if s % 4 < 3:
                dwqkv[where, s % 4 * D:s % 4 * D + D] = block[s].astype(F32)
            else:
                dwout[where, :] = block[s].astype(F32)

    write(core, gathered.at[0])
    wait(gathered.at[1], dw_sem.at[9])
    write(1 - core, gathered.at[1])

    for c in range(PARTS):
        wait(staged.at[c], go_sem.at[c])
    wait(leaving, back_sem)
    wait(leaving, land_sem)
    wait(away.at[0], dw_sem.at[0])
    wait(terms, dw_sem.at[2])
    wait(gathered.at[0], dw_sem.at[6])
    wait(gathered.at[0], dw_sem.at[8])


def body(tokens, grad_out, w_qkv, w_out):
    shape = (MEM, PARTS, WIN, D)
    hbm, anywhere, vmem = (pl.BlockSpec(memory_space=space) for space in (pltpu.HBM, pl.ANY, pltpu.VMEM))
    out, dwqkv, dwout = pl.pallas_call(
        kernel,
        out_shape=(jax.ShapeDtypeStruct(shape, BF), jax.ShapeDtypeStruct((D, 3 * D), F32), jax.ShapeDtypeStruct((D, D), F32)),
        in_specs=[hbm, hbm, hbm, hbm],
        out_specs=(anywhere, vmem, vmem),
        scratch_shapes=[
            pltpu.VMEM((PARTS, MEM, WIN, 2 * D), BF),
            pltpu.VMEM((PARTS, MEM, WIN, 2 * D), BF),
            pltpu.VMEM((PARTS, MEM, WIN, D), BF),
            pltpu.VMEM((D, 3 * D), BF),
            pltpu.VMEM((D, D), BF),
            pltpu.VMEM((256, 256), BF),
            pltpu.VMEM((WIN, MEM, D), BF),
            pltpu.VMEM((WIN, MEM, D), BF),
            pltpu.VMEM((WIN, MEM, 4 * D), BF),
            pltpu.VMEM((WIN, MEM, 3 * D), BF),
            pltpu.VMEM((WIN, MEM, D), BF),
            pltpu.VMEM((WIN, MEM, D), BF),
            pltpu.VMEM((STEP, 2, 2, MEM, 256), F32),
            pltpu.VMEM((STEP, 2, 2 * MEM, 256), BF),
            pltpu.VMEM((D, 4 * D), F32),
            pltpu.VMEM((2, D // 2, 4 * D), BF),
            pltpu.VMEM((CHIPS + 1, 16, D), BF),
            pltpu.VMEM((CHIPS, 16, D), BF),
            pltpu.VMEM((16, D), F32),
            pltpu.VMEM((16, D), F32),
            pltpu.VMEM((2, CHIPS, 16, D), BF),
            pltpu.SemaphoreType.DMA((PARTS, 2)),
            pltpu.SemaphoreType.DMA((2,)),
            pltpu.SemaphoreType.DMA((PARTS,)),
            pltpu.SemaphoreType.DMA((PARTS,)),
            pltpu.SemaphoreType.DMA(()),
            pltpu.SemaphoreType.DMA(()),
            pltpu.SemaphoreType.DMA((10,)),
        ],
        compiler_params=pltpu.CompilerParams(collective_id=0, has_side_effects=True, vmem_limit_bytes=48 << 20),
        name="grid_attention_backward",
    )(*(pltpu.with_memory_space_constraint(a, pltpu.HBM) for a in (tokens.reshape(shape), grad_out.reshape(shape), w_qkv, w_out)))
    return out.reshape(tokens.shape), dwqkv, dwout


def solution(mesh):
    spec = P("gx", "gy", "gz", None)
    return jax.shard_map(body, mesh=mesh, in_specs=(spec, spec, P(), P()), out_specs=(spec, P(), P()), check_vma=False)
```

```python
import functools
import math

import jax
import jax.numpy as jnp
from jax import lax
from jax.experimental import pallas as pl
from jax.experimental.pallas import tpu as pltpu
from jax.sharding import PartitionSpec as P

BF = jnp.bfloat16
F32 = jnp.float32
LOGICAL = pl.DeviceIdType.LOGICAL
HD = 32
MEM = 64
WIN = 16
PARTS = 4
STEP = 2
CHIPS = 32
D = 256
NN = (((1,), (0,)), ((), ()))
NT = (((1,), (1,)), ((), ()))
TN = (((0,), (0,)), ((), ()))
SCALE = HD ** -0.5


def dot(a, b, dims=NN):
    return lax.dot_general(a, b, dims, preferred_element_type=F32)


def swap_matrix():
    row = lax.broadcasted_iota(jnp.int32, (256, 256), 0)
    col = lax.broadcasted_iota(jnp.int32, (256, 256), 1)
    return jnp.where((row % 16) * 16 + row // 16 == col, 1.0, 0.0).astype(BF)


def spread(rows):
    lane = lax.broadcasted_iota(jnp.int32, (MEM, 128), 1) // HD
    return jnp.concatenate([jnp.where(lane == h, rows, jnp.zeros_like(rows)) for h in range(4)], axis=0)


def gather_heads(wide):
    lane = lax.broadcasted_iota(jnp.int32, (MEM, 128), 1) // HD
    out = wide[3 * MEM:]
    for h in (2, 1, 0):
        out = jnp.where(lane == h, wide[h * MEM:(h + 1) * MEM], out)
    return out


def columns(hg):
    return [slice(b * D + hg * 128, b * D + hg * 128 + 128) for b in range(4)]


def stage1(w, qkvg, sbuf):
    for hg in range(2):
        q, k, v, g = (qkvg[w, :, s] for s in columns(hg))
        sbuf[0, hg] = dot(k, spread(q), NT)
        sbuf[1, hg] = dot(v, spread(g), NT)


def stage2(sbuf, pbuf):
    for hg in range(2):
        scores = sbuf[0, hg]
        top = jnp.max(scores, axis=0, keepdims=True)
        e = jnp.exp2((scores - top) * (SCALE * math.log2(math.e)))
        total = jnp.sum(e, axis=0, keepdims=True)
        att = e * (1.0 / total)
        wg = sbuf[1, hg]
        inner = jnp.sum(att * wg, axis=0, keepdims=True)
        pbuf[hg, :MEM] = att.astype(BF)
        pbuf[hg, MEM:] = (att * ((wg - inner) * SCALE)).astype(BF)


def stage3(w, qkvg, pbuf, mix, grads):
    for hg in range(2):
        s = columns(hg)
        q, k, v, g = (qkvg[w, :, part] for part in s)
        both = pbuf[hg]
        rows = dot(both, jnp.concatenate([spread(g), spread(q)], axis=1))
        grads[w, :, s[2]] = rows[:MEM, :128].astype(BF)
        grads[w, :, s[1]] = rows[MEM:, 128:].astype(BF)
        zero = jnp.zeros_like(v)
        vk = jnp.concatenate([jnp.concatenate([v, zero], axis=1), jnp.concatenate([zero, k], axis=1)], axis=0)
        wide = dot(both, vk, TN)
        mix[w, :, s[0]] = gather_heads(wide[:, :128]).astype(BF)
        grads[w, :, s[0]] = gather_heads(wide[:, 128:]).astype(BF)


def attend(arrived, swap, wqkv, wout, xw, gw, qkvg, grads, mix, sbuf, pbuf, acc):
    for m in range(0, MEM, 16):
        rows = dot(swap[...], arrived[m:m + 16].reshape(256, 512)).astype(BF).reshape(WIN, 16, 512)
        xw[:, m:m + 16, :] = rows[:, :, :D]
        gw[:, m:m + 16, :] = rows[:, :, D:]

    x = xw[...].reshape(-1, D)
    g = gw[...].reshape(-1, D)
    qkvg[:, :, 0:3 * D] = dot(x, wqkv[...]).astype(BF).reshape(WIN, MEM, 3 * D)
    qkvg[:, :, 3 * D:] = dot(g, wout[...], NT).astype(BF).reshape(WIN, MEM, D)

    last = WIN // STEP - 1

    def step(i, carry):
        for u in range(STEP):
            stage3(jnp.maximum(i - 2, 0) * STEP + u, qkvg, pbuf.at[u], mix, grads)
        for u in range(STEP):
            stage2(sbuf.at[u], pbuf.at[u])
        for u in range(STEP):
            stage1(jnp.minimum(i, last) * STEP + u, qkvg, sbuf.at[u])
        return carry

    lax.fori_loop(0, last + 3, step, 0)

    acc[:, 0:3 * D] += dot(xw[...].reshape(-1, D), grads[...].reshape(-1, 3 * D), TN)
    acc[:, 3 * D:] += dot(mix[...].reshape(-1, D), gw[...].reshape(-1, D), TN)


def token_gradients(leaving, swap, wqkv, grads, dx):
    dx[...] = dot(grads[...].reshape(-1, 3 * D), wqkv[...], NT).astype(BF).reshape(WIN, MEM, D)
    for m in range(0, MEM, 16):
        rows = dx[:, m:m + 16, :].reshape(256, D)
        leaving[m:m + 16] = dot(swap[...], rows).astype(BF).reshape(16, WIN, D)


def kernel(tok, grd, wqkv_hbm, wout_hbm, out, gathered, staged, arrived, leaving, wqkv, wout, swap, xw, gw, qkvg, grads,
           mix, dx, sbuf, pbuf, acc, away, home, terms, half, pair,
           stage_sem, weight_sem, go_sem, come_sem, back_sem, land_sem, dw_sem):
    y, gy, gz = lax.axis_index("gx"), lax.axis_index("gy"), lax.axis_index("gz")
    x_hi, core = gy // 2, gy % 2
    x, z_hi, z_lo = x_hi * 2 + gz // 4, gz % 4 // 2, gz % 2
    chip = y * 8 + x * 2 + z_hi
    me = chip * 2 + core

    def device(y_of, x_of, z_of, core_of, z_low):
        return y_of * 32 + x_of // 2 * 16 + core_of * 8 + x_of % 2 * 4 + z_of * 2 + z_low

    ys = tuple((y + d) % 4 for d in range(4))
    xs = tuple((x + d) % 4 for d in range(4))
    ends = tuple(((z_hi + e) % 2, (core + e // 2) % 2) for e in range(4))
    y_part = tuple(v * 16 for v in ys)
    x_part = tuple((v * 4, device(0, v, 0, 0, 1 - z_lo)) for v in xs)
    end_part = tuple((z_of * 2 + core_of, device(0, 0, z_of, core_of, 0)) for z_of, core_of in ends)

    def for_partners(act, first=0, last=4):
        def outer(k, e_carry):
            def inner(i, carry):
                y_carry, e_now = carry
                for d in range(4):
                    y_of, (x_num, x_dev), (e_num, e_dev) = y_carry[d], x_part[d], e_now[d]
                    act(y_of + x_num + e_num, y_of * 2 + x_dev + e_dev)
                return y_carry[1:] + y_carry[:1], e_now[-1:] + e_now[:-1]
            lax.fori_loop(0, 4, inner, (y_part, e_carry))
            return e_carry[1:] + e_carry[:1]
        lax.fori_loop(first, last, outer, end_part[first:] + end_part[:first])

    def for_chips(act):
        def outer(i, y_carry):
            for d in (2, 1, 3, 0):
                for z_of in (z_hi, 1 - z_hi):
                    y_of, (x_num, x_dev) = y_carry[d], x_part[d]
                    act((y_of + x_num) // 2 + z_of, y_of * 2 + x_dev + device(0, 0, z_of, core, 0))
            return y_carry[1:] + y_carry[:1]
        lax.fori_loop(0, 4, outer, y_part)

    other_core = device(y, x, z_hi, 1 - core, z_lo)
    across = device(y, x, z_hi, core, 1 - z_lo)

    def send(src, dst, send_sem, recv_sem, to):
        copy = pltpu.make_async_remote_copy(src, dst, send_sem, recv_sem, device_id=to, device_id_type=LOGICAL)
        copy.start()
        return copy

    def wait(ref, sem):
        pltpu.make_async_copy(ref, ref, sem).wait()

    barrier = pltpu.get_barrier_semaphore()
    for_partners(lambda t, to: pl.semaphore_signal(barrier, inc=1, device_id=to, device_id_type=LOGICAL))
    pl.semaphore_signal(barrier, inc=1, device_id=other_core, device_id_type=LOGICAL)
    stagings = []
    for c in range(PARTS):
        for k, ref in enumerate((tok, grd)):
            copy = pltpu.make_async_copy(ref.at[:, c], staged.at[c, :, :, pl.ds(k * D, D)], stage_sem.at[c, k])
            copy.start()
            stagings.append(copy)
    weights = [pltpu.make_async_copy(wqkv_hbm, wqkv, weight_sem.at[0]), pltpu.make_async_copy(wout_hbm, wout, weight_sem.at[1])]
    for copy in weights:
        copy.start()

    swap[...] = swap_matrix()
    acc[...] = jnp.zeros_like(acc)
    pl.semaphore_wait(barrier, MEM + 1)

    for c in range(PARTS):
        stagings[2 * c].wait()
        stagings[2 * c + 1].wait()
        for_partners(lambda t, to: send(staged.at[c, t], arrived.at[c, me], go_sem.at[c], come_sem.at[c], to))
    for copy in weights:
        copy.wait()

    def send_back(c, first=0, last=4):
        for_partners(lambda t, to: send(leaving.at[c, t], out.at[me, c], back_sem, land_sem, to), first, last)

    rows = D // 2
    first, second = pl.ds(pl.multiple_of(core * rows, rows), rows), pl.ds(pl.multiple_of((1 - core) * rows, rows), rows)

    def part(c, carry):
        wait(arrived.at[c], come_sem.at[c])
        attend(arrived.at[c], swap, wqkv, wout, xw, gw, qkvg, grads, mix, sbuf, pbuf, acc)

        @pl.when(c == PARTS - 1)
        def _():
            away[0] = acc[second, :].astype(BF)
            send(away.at[0], away.at[1], dw_sem.at[0], dw_sem.at[1], other_core)

        token_gradients(leaving.at[c], swap, wqkv, grads, dx)

        @pl.when(c == PARTS - 1)
        def _():
            wait(away.at[1], dw_sem.at[1])
            both = (acc[first, :] + away[1].astype(F32)).astype(BF)
            for s in range(CHIPS):
                home[s] = both[s // 4 * 16:s // 4 * 16 + 16, s % 4 * D:s % 4 * D + D]
            for_chips(lambda t, to: send(home.at[t], terms.at[chip], dw_sem.at[2], dw_sem.at[3], to))
            send_back(2, 2, 4)
            send_back(3, 0, 1)

        @pl.when(c == 0)
        def _():
            send_back(0, 0, 4)

        @pl.when(c == 1)
        def _():
            send_back(1, 0, 3)

        @pl.when(c == 2)
        def _():
            send_back(1, 3, 4)
            send_back(2, 0, 2)

        return carry

    lax.fori_loop(0, PARTS, part, 0)

    wait(terms, dw_sem.at[3])
    total = terms[0].astype(F32)
    for s in range(1, CHIPS):
        total += terms[s].astype(F32)
    half[...] = total
    exchange = send(half, pair, dw_sem.at[4], dw_sem.at[5], across)
    send_back(3, 1, 2)
    exchange.wait()
    block = (pl.ds(pl.multiple_of(core * rows + chip // 4 * 16, 16), 16), pl.ds(pl.multiple_of(chip % 4 * D, D), D))
    mine = home.at[CHIPS]
    mine[...] = (half[...] + pair[...]).astype(BF)
    for_chips(lambda t, to: send(mine, gathered.at[block], dw_sem.at[6], dw_sem.at[7], to))
    send_back(3, 2, 4)
    wait(terms, dw_sem.at[7])
    send(gathered.at[first], gathered.at[first], dw_sem.at[8], dw_sem.at[9], other_core)

    for c in range(PARTS):
        wait(staged.at[c], go_sem.at[c])
    wait(leaving, back_sem)
    wait(leaving, land_sem)
    wait(away.at[0], dw_sem.at[0])
    wait(terms, dw_sem.at[2])
    wait(terms, dw_sem.at[6])
    wait(terms, dw_sem.at[8])
    wait(terms, dw_sem.at[9])


def body(tokens, grad_out, w_qkv, w_out):
    shape = (MEM, PARTS, WIN, D)
    hbm, anywhere, vmem = (pl.BlockSpec(memory_space=space) for space in (pltpu.HBM, pl.ANY, pltpu.VMEM))
    out, gathered = pl.pallas_call(
        kernel,
        out_shape=(jax.ShapeDtypeStruct(shape, BF), jax.ShapeDtypeStruct((D, 4 * D), BF)),
        in_specs=[hbm, hbm, hbm, hbm],
        out_specs=(anywhere, vmem),
        scratch_shapes=[
            pltpu.VMEM((PARTS, MEM, WIN, 2 * D), BF),
            pltpu.VMEM((PARTS, MEM, WIN, 2 * D), BF),
            pltpu.VMEM((PARTS, MEM, WIN, D), BF),
            pltpu.VMEM((D, 3 * D), BF),
            pltpu.VMEM((D, D), BF),
            pltpu.VMEM((256, 256), BF),
            pltpu.VMEM((WIN, MEM, D), BF),
            pltpu.VMEM((WIN, MEM, D), BF),
            pltpu.VMEM((WIN, MEM, 4 * D), BF),
            pltpu.VMEM((WIN, MEM, 3 * D), BF),
            pltpu.VMEM((WIN, MEM, D), BF),
            pltpu.VMEM((WIN, MEM, D), BF),
            pltpu.VMEM((STEP, 2, 2, MEM, 256), F32),
            pltpu.VMEM((STEP, 2, 2 * MEM, 256), BF),
            pltpu.VMEM((D, 4 * D), F32),
            pltpu.VMEM((2, D // 2, 4 * D), BF),
            pltpu.VMEM((CHIPS + 1, 16, D), BF),
            pltpu.VMEM((CHIPS, 16, D), BF),
            pltpu.VMEM((16, D), F32),
            pltpu.VMEM((16, D), F32),
            pltpu.SemaphoreType.DMA((PARTS, 2)),
            pltpu.SemaphoreType.DMA((2,)),
            pltpu.SemaphoreType.DMA((PARTS,)),
            pltpu.SemaphoreType.DMA((PARTS,)),
            pltpu.SemaphoreType.DMA(()),
            pltpu.SemaphoreType.DMA(()),
            pltpu.SemaphoreType.DMA((10,)),
        ],
        compiler_params=pltpu.CompilerParams(collective_id=0, has_side_effects=True, vmem_limit_bytes=48 << 20),
        name="grid_attention_backward",
    )(*(pltpu.with_memory_space_constraint(a, pltpu.HBM) for a in (tokens.reshape(shape), grad_out.reshape(shape), w_qkv, w_out)))
    return out.reshape(tokens.shape), gathered[:, :3 * D].astype(F32), gathered[:, 3 * D:].astype(F32)


def solution(mesh):
    spec = P("gx", "gy", "gz", None)
    return jax.shard_map(body, mesh=mesh, in_specs=(spec, spec, P(), P()), out_specs=(spec, P(), P()), check_vma=False)
```

```python
import functools
import math

import jax
import jax.numpy as jnp
from jax import lax
from jax.experimental import pallas as pl
from jax.experimental.pallas import tpu as pltpu
from jax.sharding import PartitionSpec as P

BF = jnp.bfloat16
F32 = jnp.float32
LOGICAL = pl.DeviceIdType.LOGICAL
HD = 32
MEM = 64
WIN = 16
PARTS = 4
STEP = 2
CHIPS = 32
D = 256
NN = (((1,), (0,)), ((), ()))
NT = (((1,), (1,)), ((), ()))
TN = (((0,), (0,)), ((), ()))
SCALE = HD ** -0.5


def dot(a, b, dims=NN):
    return lax.dot_general(a, b, dims, preferred_element_type=F32)


def swap_matrix():
    row = lax.broadcasted_iota(jnp.int32, (256, 256), 0)
    col = lax.broadcasted_iota(jnp.int32, (256, 256), 1)
    return jnp.where((row % 16) * 16 + row // 16 == col, 1.0, 0.0).astype(BF)


def spread(rows):
    lane = lax.broadcasted_iota(jnp.int32, (MEM, 128), 1) // HD
    return jnp.concatenate([jnp.where(lane == h, rows, jnp.zeros_like(rows)) for h in range(4)], axis=0)


def gather_heads(wide):
    lane = lax.broadcasted_iota(jnp.int32, (MEM, 128), 1) // HD
    out = wide[3 * MEM:]
    for h in (2, 1, 0):
        out = jnp.where(lane == h, wide[h * MEM:(h + 1) * MEM], out)
    return out


def columns(hg):
    return [slice(b * D + hg * 128, b * D + hg * 128 + 128) for b in range(4)]


def stage1(w, qkvg, sbuf):
    for hg in range(2):
        q, k, v, g = (qkvg[w, :, s] for s in columns(hg))
        sbuf[0, hg] = dot(k, spread(q), NT)
        sbuf[1, hg] = dot(v, spread(g), NT)


def stage2(sbuf, pbuf):
    for hg in range(2):
        scores = sbuf[0, hg]
        top = jnp.max(scores, axis=0, keepdims=True)
        e = jnp.exp2((scores - top) * (SCALE * math.log2(math.e)))
        total = jnp.sum(e, axis=0, keepdims=True)
        att = e * (1.0 / total)
        wg = sbuf[1, hg]
        inner = jnp.sum(att * wg, axis=0, keepdims=True)
        pbuf[hg, :MEM] = att.astype(BF)
        pbuf[hg, MEM:] = (att * ((wg - inner) * SCALE)).astype(BF)


def stage3(w, qkvg, pbuf, mix, grads):
    for hg in range(2):
        s = columns(hg)
        q, k, v, g = (qkvg[w, :, part] for part in s)
        both = pbuf[hg]
        rows = dot(both, jnp.concatenate([spread(g), spread(q)], axis=1))
        grads[w, :, s[2]] = rows[:MEM, :128].astype(BF)
        grads[w, :, s[1]] = rows[MEM:, 128:].astype(BF)
        zero = jnp.zeros_like(v)
        vk = jnp.concatenate([jnp.concatenate([v, zero], axis=1), jnp.concatenate([zero, k], axis=1)], axis=0)
        wide = dot(both, vk, TN)
        mix[w, :, s[0]] = gather_heads(wide[:, :128]).astype(BF)
        grads[w, :, s[0]] = gather_heads(wide[:, 128:]).astype(BF)


def attend(arrived, swap, wqkv, wout, xw, gw, qkvg, grads, mix, sbuf, pbuf, acc):
    for m in range(0, MEM, 16):
        rows = dot(swap[...], arrived[m:m + 16].reshape(256, 512)).astype(BF).reshape(WIN, 16, 512)
        xw[:, m:m + 16, :] = rows[:, :, :D]
        gw[:, m:m + 16, :] = rows[:, :, D:]

    x = xw[...].reshape(-1, D)
    g = gw[...].reshape(-1, D)
    qkvg[:, :, 0:3 * D] = dot(x, wqkv[...]).astype(BF).reshape(WIN, MEM, 3 * D)
    qkvg[:, :, 3 * D:] = dot(g, wout[...], NT).astype(BF).reshape(WIN, MEM, D)

    last = WIN // STEP - 1

    def step(i, carry):
        for u in range(STEP):
            stage3(jnp.maximum(i - 2, 0) * STEP + u, qkvg, pbuf.at[u], mix, grads)
        for u in range(STEP):
            stage2(sbuf.at[u], pbuf.at[u])
        for u in range(STEP):
            stage1(jnp.minimum(i, last) * STEP + u, qkvg, sbuf.at[u])
        return carry

    lax.fori_loop(0, last + 3, step, 0)

    acc[:, 0:3 * D] += dot(xw[...].reshape(-1, D), grads[...].reshape(-1, 3 * D), TN)
    acc[:, 3 * D:] += dot(mix[...].reshape(-1, D), gw[...].reshape(-1, D), TN)


def token_gradients(leaving, swap, wqkv, grads, dx):
    dx[...] = dot(grads[...].reshape(-1, 3 * D), wqkv[...], NT).astype(BF).reshape(WIN, MEM, D)
    for m in range(0, MEM, 16):
        rows = dx[:, m:m + 16, :].reshape(256, D)
        leaving[m:m + 16] = dot(swap[...], rows).astype(BF).reshape(16, WIN, D)


def kernel(tok, grd, wqkv_hbm, wout_hbm, out, dwqkv, dwout, staged, arrived, leaving, wqkv, wout, swap, xw, gw, qkvg, grads,
           mix, dx, sbuf, pbuf, acc, away, home, terms, half, pair, gathered,
           stage_sem, weight_sem, go_sem, come_sem, back_sem, land_sem, dw_sem, gather_sem):
    y, gy, gz = lax.axis_index("gx"), lax.axis_index("gy"), lax.axis_index("gz")
    x_hi, core = gy // 2, gy % 2
    x, z_hi, z_lo = x_hi * 2 + gz // 4, gz % 4 // 2, gz % 2
    chip = y * 8 + x * 2 + z_hi
    me = chip * 2 + core

    def device(y_of, x_of, z_of, core_of, z_low):
        return y_of * 32 + x_of // 2 * 16 + core_of * 8 + x_of % 2 * 4 + z_of * 2 + z_low

    ys = tuple((y + d) % 4 for d in range(4))
    xs = tuple((x + d) % 4 for d in range(4))
    ends = tuple(((z_hi + e) % 2, (core + e // 2) % 2) for e in range(4))
    y_part = tuple(v * 16 for v in ys)
    x_part = tuple((v * 4, device(0, v, 0, 0, 1 - z_lo)) for v in xs)
    end_part = tuple((z_of * 2 + core_of, device(0, 0, z_of, core_of, 0)) for z_of, core_of in ends)

    def for_partners(act, first=0, last=4):
        def outer(k, e_carry):
            def inner(i, carry):
                y_carry, e_now = carry
                for d in range(4):
                    y_of, (x_num, x_dev), (e_num, e_dev) = y_carry[d], x_part[d], e_now[d]
                    act(y_of + x_num + e_num, y_of * 2 + x_dev + e_dev)
                return y_carry[1:] + y_carry[:1], e_now[-1:] + e_now[:-1]
            lax.fori_loop(0, 4, inner, (y_part, e_carry))
            return e_carry[1:] + e_carry[:1]
        lax.fori_loop(first, last, outer, end_part[first:] + end_part[:first])

    def for_chips(act):
        def outer(i, y_carry):
            for d in range(4):
                for z_of in (z_hi, 1 - z_hi):
                    y_of, (x_num, x_dev) = y_carry[d], x_part[d]
                    act((y_of + x_num) // 2 + z_of, y_of * 2 + x_dev + device(0, 0, z_of, core, 0), i)
            return y_carry[1:] + y_carry[:1]
        lax.fori_loop(0, 4, outer, y_part)

    other_core = device(y, x, z_hi, 1 - core, z_lo)
    across = device(y, x, z_hi, core, 1 - z_lo)

    def send(src, dst, send_sem, recv_sem, to):
        copy = pltpu.make_async_remote_copy(src, dst, send_sem, recv_sem, device_id=to, device_id_type=LOGICAL)
        copy.start()
        return copy

    def wait(ref, sem):
        pltpu.make_async_copy(ref, ref, sem).wait()

    barrier = pltpu.get_barrier_semaphore()
    for_partners(lambda t, to: pl.semaphore_signal(barrier, inc=1, device_id=to, device_id_type=LOGICAL))
    pl.semaphore_signal(barrier, inc=1, device_id=other_core, device_id_type=LOGICAL)
    stagings = []
    for c in range(PARTS):
        for k, ref in enumerate((tok, grd)):
            copy = pltpu.make_async_copy(ref.at[:, c], staged.at[c, :, :, pl.ds(k * D, D)], stage_sem.at[c, k])
            copy.start()
            stagings.append(copy)
    weights = [pltpu.make_async_copy(wqkv_hbm, wqkv, weight_sem.at[0]), pltpu.make_async_copy(wout_hbm, wout, weight_sem.at[1])]
    for copy in weights:
        copy.start()

    swap[...] = swap_matrix()
    acc[...] = jnp.zeros_like(acc)
    pl.semaphore_wait(barrier, MEM + 1)

    for c in range(PARTS):
        stagings[2 * c].wait()
        stagings[2 * c + 1].wait()
        for_partners(lambda t, to: send(staged.at[c, t], arrived.at[c, me], go_sem.at[c], come_sem.at[c], to))
    for copy in weights:
        copy.wait()

    def send_back(c, first=0, last=4):
        for_partners(lambda t, to: send(leaving.at[c, t], out.at[me, c], back_sem, land_sem, to), first, last)

    rows = D // 2
    first, second = pl.ds(pl.multiple_of(core * rows, rows), rows), pl.ds(pl.multiple_of((1 - core) * rows, rows), rows)

    def part(c, carry):
        wait(arrived.at[c], come_sem.at[c])
        attend(arrived.at[c], swap, wqkv, wout, xw, gw, qkvg, grads, mix, sbuf, pbuf, acc)

        @pl.when(c == PARTS - 1)
        def _():
            away[0] = acc[second, :].astype(BF)
            send(away.at[0], away.at[1], dw_sem.at[0], dw_sem.at[1], other_core)

        token_gradients(leaving.at[c], swap, wqkv, grads, dx)

        @pl.when(c == PARTS - 1)
        def _():
            wait(away.at[1], dw_sem.at[1])
            both = (acc[first, :] + away[1].astype(F32)).astype(BF)
            for s in range(CHIPS):
                home[s] = both[s // 4 * 16:s // 4 * 16 + 16, s % 4 * D:s % 4 * D + D]
            for_chips(lambda t, to, i: send(home.at[t], terms.at[chip], dw_sem.at[2], dw_sem.at[3], to))
            send_back(2, 2, 4)
            send_back(3, 0, 1)

        @pl.when(c == 0)
        def _():
            send_back(0, 0, 4)

        @pl.when(c == 1)
        def _():
            send_back(1, 0, 3)

        @pl.when(c == 2)
        def _():
            send_back(1, 3, 4)
            send_back(2, 0, 2)

        return carry

    lax.fori_loop(0, PARTS, part, 0)

    wait(terms, dw_sem.at[3])
    total = terms[0].astype(F32)
    for s in range(1, CHIPS):
        total += terms[s].astype(F32)
    half[...] = total
    exchange = send(half, pair, dw_sem.at[4], dw_sem.at[5], across)
    send_back(3, 1, 2)
    exchange.wait()
    mine = home.at[CHIPS]
    mine[...] = (half[...] + pair[...]).astype(BF)
    for_chips(lambda t, to, i: send(mine, gathered.at[0, chip], dw_sem.at[6], gather_sem.at[i], to))
    send_back(3, 2, 4)
    for i in range(4):
        wait(gathered.at[0, pl.ds(0, CHIPS // 4)], gather_sem.at[i])
        for d in range(4):
            chips = pl.ds((y_part[(-d - i) % 4] + x_part[-d % 4][0]) // 2, 2)
            send(gathered.at[0, chips], gathered.at[1, chips], dw_sem.at[7], dw_sem.at[8], other_core)

    def write(owner, block):
        for s in range(CHIPS):
            where = pl.ds(pl.multiple_of(owner * rows + s // 4 * 16, 16), 16)
            if s % 4 < 3:
                dwqkv[where, s % 4 * D:s % 4 * D + D] = block[s].astype(F32)
            else:
                dwout[where, :] = block[s].astype(F32)

    write(core, gathered.at[0])
    wait(gathered.at[1], dw_sem.at[8])
    write(1 - core, gathered.at[1])

    for c in range(PARTS):
        wait(staged.at[c], go_sem.at[c])
    wait(leaving, back_sem)
    wait(leaving, land_sem)
    wait(away.at[0], dw_sem.at[0])
    wait(terms, dw_sem.at[2])
    wait(gathered.at[0], dw_sem.at[6])
    wait(gathered.at[0], dw_sem.at[7])


def body(tokens, grad_out, w_qkv, w_out):
    shape = (MEM, PARTS, WIN, D)
    hbm, anywhere, vmem = (pl.BlockSpec(memory_space=space) for space in (pltpu.HBM, pl.ANY, pltpu.VMEM))
    out, dwqkv, dwout = pl.pallas_call(
        kernel,
        out_shape=(jax.ShapeDtypeStruct(shape, BF), jax.ShapeDtypeStruct((D, 3 * D), F32), jax.ShapeDtypeStruct((D, D), F32)),
        in_specs=[hbm, hbm, hbm, hbm],
        out_specs=(anywhere, vmem, vmem),
        scratch_shapes=[
            pltpu.VMEM((PARTS, MEM, WIN, 2 * D), BF),
            pltpu.VMEM((PARTS, MEM, WIN, 2 * D), BF),
            pltpu.VMEM((PARTS, MEM, WIN, D), BF),
            pltpu.VMEM((D, 3 * D), BF),
            pltpu.VMEM((D, D), BF),
            pltpu.VMEM((256, 256), BF),
            pltpu.VMEM((WIN, MEM, D), BF),
            pltpu.VMEM((WIN, MEM, D), BF),
            pltpu.VMEM((WIN, MEM, 4 * D), BF),
            pltpu.VMEM((WIN, MEM, 3 * D), BF),
            pltpu.VMEM((WIN, MEM, D), BF),
            pltpu.VMEM((WIN, MEM, D), BF),
            pltpu.VMEM((STEP, 2, 2, MEM, 256), F32),
            pltpu.VMEM((STEP, 2, 2 * MEM, 256), BF),
            pltpu.VMEM((D, 4 * D), F32),
            pltpu.VMEM((2, D // 2, 4 * D), BF),
            pltpu.VMEM((CHIPS + 1, 16, D), BF),
            pltpu.VMEM((CHIPS, 16, D), BF),
            pltpu.VMEM((16, D), F32),
            pltpu.VMEM((16, D), F32),
            pltpu.VMEM((2, CHIPS, 16, D), BF),
            pltpu.SemaphoreType.DMA((PARTS, 2)),
            pltpu.SemaphoreType.DMA((2,)),
            pltpu.SemaphoreType.DMA((PARTS,)),
            pltpu.SemaphoreType.DMA((PARTS,)),
            pltpu.SemaphoreType.DMA(()),
            pltpu.SemaphoreType.DMA(()),
            pltpu.SemaphoreType.DMA((9,)),
            pltpu.SemaphoreType.DMA((4,)),
        ],
        compiler_params=pltpu.CompilerParams(collective_id=0, has_side_effects=True, vmem_limit_bytes=48 << 20),
        name="grid_attention_backward",
    )(*(pltpu.with_memory_space_constraint(a, pltpu.HBM) for a in (tokens.reshape(shape), grad_out.reshape(shape), w_qkv, w_out)))
    return out.reshape(tokens.shape), dwqkv, dwout


def solution(mesh):
    spec = P("gx", "gy", "gz", None)
    return jax.shard_map(body, mesh=mesh, in_specs=(spec, spec, P(), P()), out_specs=(spec, P(), P()), check_vma=False)
```
